32 devices in a mesh: wide: 8 (over z, y), narrow: 4 (over x, core).
Axes of the slice: x: 2, y: 2, z: 4, core: 2. Of those that a mesh axis runs over, the one named last changes fastest.
Arguments:
- tokens: bfloat16 [32, 1024, 1024], P(('wide', 'narrow')), may hold values from -6 to 6
- lengths: int32 [32, 2], P(('wide', 'narrow')), may hold values from 316 to 1024, as said below
- latents: bfloat16 [512, 1024], replicated, may hold values from -6 to 6
- norm_gain: float32 [4, 1024], replicated, may hold values from 0.1 to 1.9
- norm_bias: float32 [4, 1024], replicated, may hold values from -1.8 to 1.8
- cross_qkv: bfloat16 [3, 1024, 1024], replicated, may hold values from -0.1875 to 0.1875
- cross_out: bfloat16 [1024, 1024], replicated, may hold values from -3 to 3
- self_qkv: bfloat16 [3, 1024, 1024], replicated, may hold values from -0.1875 to 0.1875
- self_out: bfloat16 [1024, 1024], replicated, may hold values from -3 to 3
- mlp_in: bfloat16 [1024, 4096], replicated, may hold values from -0.1875 to 0.1875
- mlp_biases: float32 [5120], replicated, may hold values from -2.4 to 2.4
- mlp_out: bfloat16 [4096, 1024], replicated, may hold values from -0.09375 to 0.09375
- cotangent: bfloat16 [32, 512, 1024], P(('wide', 'narrow')), may hold values from -6 to 6
Outputs:
- latents_out: bfloat16 [32, 512, 1024], P(('wide', 'narrow'))
- tokens_grad: float32 [32, 1024, 1024], P(('wide', 'narrow'))
- latents_grad: float32 [512, 1024], P('narrow', 'wide')
- gain_grad: float32 [4, 1024], P('narrow', 'wide')
- bias_grad: float32 [4, 1024], P('narrow', 'wide')
- cross_qkv_grad: float32 [3, 1024, 1024], P(None, 'narrow', 'wide')
- cross_out_grad: float32 [1024, 1024], P('narrow', 'wide')
- self_qkv_grad: float32 [3, 1024, 1024], P(None, 'narrow', 'wide')
- self_out_grad: float32 [1024, 1024], P('narrow', 'wide')
- mlp_in_grad: float32 [1024, 4096], P('narrow', 'wide')
- mlp_biases_grad: float32 [5120], P(('wide', 'narrow'))
- mlp_out_grad: float32 [4096, 1024], P('narrow', 'wide')
The draws below stay inside these ranges and needn't reach their ends.
Inputs may be any that keep to these rules, and one draw needn't show every extreme that they name: lengths[g, s] counts the valid leading rows of image s of the merged groups of g and its partner, and is the same on both; it is one of 1024, 619 and (26214400) // 82944 (images of 288, 224 and 160 pixels); in every pair one of the two images has 288 pixels.
All inputs are finite; a program needn't handle non-finite values.
Results may differ from the reference program's by a relative error of at most 0.013.
Values may be sent and summed in bfloat16 or wider, within the bound.
No kernel may reach another device: no remote copies, remote signals or barrier semaphores. Data moves between devices by JAX's collectives and lax.ppermute only.
A program may use at most 256 MiB of HBM per device.

```python
import jax
import jax.numpy as jnp
from jax import lax

D = 1024
FF = 4096
HEADS = 8
HEAD_DIM = 128
K = 512
TOK = 512
GROUPS = 32


def draw_lengths(key, part):
    pair_count = GROUPS // 2
    class_key, pick_key = jax.random.split(jax.random.fold_in(key, 11))
    classes = jax.random.randint(class_key, (pair_count, 2), 0, 3)
    chosen = jax.random.randint(pick_key, (pair_count, 1), 0, 2)
    slot_ids = jnp.arange(2)[None, :]
    classes = jnp.where(slot_ids == chosen, 2, classes)
    larger = 2 * TOK * 50176 // 82944
    smaller = 2 * TOK * 25600 // 82944
    counts = jnp.where(classes == 2, 2 * TOK, jnp.where(classes == 1, larger, smaller))
    owners = jnp.arange(GROUPS) % pair_count
    return counts[owners].astype(jnp.int32)


def spiked(array, key, source, target, shards_of, factor):
    owner, partner = [(jnp.arange(array.shape[dim]) // (array.shape[dim] // shards_of)).reshape([-1 if axis == dim else 1 for axis in range(array.ndim)]) for dim in (source, target)]
    chosen = jax.random.permutation(key, shards_of)[partner]
    strong = (owner == chosen) | (owner == (partner + shards_of // 2) % shards_of)
    return jnp.where(strong, factor * array, array)


def block_scale(stream_key, dims, pieces, smallest, high):
    def one(dim, shards_of):
        heights = jax.random.uniform(jax.random.fold_in(jax.random.fold_in(stream_key, 6), dim), (shards_of,), jnp.float32, smallest / len(pieces), high / len(pieces))
        return jnp.repeat(jnp.exp(heights), dims[dim] // shards_of).reshape((-1,) + (1,) * (len(dims) - dim - 1))

    gain = one(*pieces[0])
    for cut in pieces[1:]:
        gain = gain * one(*cut)
    return gain


def gaussian(key, shape, scale, most, pieces=(), kind=jnp.bfloat16):
    factor_of = block_scale(key, shape, pieces, -0.22, 0.18) if pieces else 1.0
    entries = jax.random.normal(key, shape, jnp.float32) * scale * factor_of
    return jnp.minimum(jnp.maximum(entries, -most), most).astype(kind)


def heavy_noise(rng, extent, scale, limit, shards, heavy, held_as=jnp.bfloat16):
    values = scale * jax.random.normal(rng, extent, jnp.float32)
    if shards:
        values = values * block_scale(rng, extent, shards, -0.22, 0.18)
    return jnp.clip(spiked(values, jax.random.fold_in(rng, 3), *heavy), -limit, limit).astype(held_as)


def setup_inputs(seed: int = 0) -> dict:
    streams_of = jax.random.split(jax.random.key(seed), 14)
    tokens = gaussian(streams_of[0], (GROUPS, 2 * TOK, D), 1.0, 6.0, ((0, 32),))
    lengths = draw_lengths(jax.random.fold_in(streams_of[13], 71), 0)
    latents = gaussian(streams_of[2], (K, D), 1.0, 6.0)
    norm_gain = jnp.clip(1.0 + 0.18 * jax.random.normal(streams_of[3], (4, D), jnp.float32), 0.1, 1.9)
    norm_bias = gaussian(streams_of[4], (4, D), 0.3, 1.8, (), jnp.float32)
    cross_qkv = gaussian(streams_of[5], (3, D, D), D ** -0.5, 0.1875)
    cross_out = gaussian(streams_of[6], (D, D), (max(2 * D // TOK, 1)) ** -0.5, 3.0)
    self_qkv = gaussian(streams_of[7], (3, D, D), D ** -0.5, 0.1875)
    self_out = gaussian(streams_of[8], (D, D), (max(2 * D // K, 1)) ** -0.5, 3.0)
    mlp_in = gaussian(streams_of[9], (D, FF), D ** -0.5, 0.1875)
    mlp_biases = gaussian(streams_of[10], (FF + D,), 0.4, 2.4, (), jnp.float32)
    mlp_out = gaussian(streams_of[11], (FF, D), FF ** -0.5, 0.09375)
    cotangent = heavy_noise(streams_of[12], (GROUPS, K, D), 1.0, 6.0, ((0, 32),), (0, 2, 32, 2.75))
    return {"tokens": tokens, "lengths": lengths, "latents": latents, "norm_gain": norm_gain, "norm_bias": norm_bias, "cross_qkv": cross_qkv, "cross_out": cross_out, "self_qkv": self_qkv, "self_out": self_out, "mlp_in": mlp_in, "mlp_biases": mlp_biases, "mlp_out": mlp_out, "cotangent": cotangent}


HIGHEST = lax.Precision.HIGHEST

@jax.custom_vjp
def low(v):
    return lax.optimization_barrier(v.astype(jnp.bfloat16)).astype(jnp.float32)

@jax.custom_vjp
def low_back(v):
    return v

def low_keep(v):
    return (low(v), None)

def low_pass(kept, grad):
    return (grad,)

def back_keep(v):
    return (v, None)

def back_low(kept, grad):
    return (low(grad),)
low.defvjp(low_keep, low_pass)
low_back.defvjp(back_keep, back_low)

def round_both(value):
    return low(low_back(value))

def product(left_side, right_side):
    return jnp.matmul(left_side, right_side, precision=HIGHEST)

def normalize(inputs, gain_row, shift_row):
    center = inputs - lax.optimization_barrier(jnp.mean(inputs, -1, keepdims=True))
    spread = lax.optimization_barrier(jnp.mean(center * center, -1, keepdims=True))
    return center * lax.rsqrt(spread + 1e-05) * gain_row + shift_row

def split_heads(matrix):
    return matrix.reshape(matrix.shape[0], HEADS, HEAD_DIM)

def attend(queries, keys_in, values_in, usable):
    factor = HEAD_DIM ** (-0.5)
    scores = low_back(jnp.einsum('qhd,khd->hqk', split_heads(queries), split_heads(keys_in), precision=HIGHEST) * factor)
    if usable is not None:
        scores = jnp.where(usable[None, None, :], scores, -1000000000.0)
    attention = jax.nn.softmax(scores, axis=-1)
    mixed = jnp.einsum('hqk,khd->qhd', low(attention), split_heads(values_in), precision=HIGHEST)
    return round_both(mixed.reshape(queries.shape[0], HEADS * HEAD_DIM))

def block_layer(rows_in, usable, latents_in, gains, shifts, cross_w, cross_o, self_w, self_o, inner_w, both_biases, outer_w):
    inner_b = both_biases[:FF]
    outer_b = both_biases[FF:]
    token_norm = low(normalize(rows_in, gains[0], shifts[0]))
    keys_in = round_both(product(token_norm, cross_w[1]))
    values_in = round_both(product(token_norm, cross_w[2]))
    latent_norm = low(normalize(latents_in, gains[1], shifts[1]))
    queries = round_both(product(latent_norm, cross_w[0]))
    first_sum = latents_in + low_back(product(attend(queries, keys_in, values_in, usable), cross_o))
    self_norm = low(normalize(first_sum, gains[2], shifts[2]))
    self_query = round_both(product(self_norm, self_w[0]))
    self_keys = round_both(product(self_norm, self_w[1]))
    self_values = round_both(product(self_norm, self_w[2]))
    second_sum = first_sum + low_back(product(attend(self_query, self_keys, self_values, None), self_o))
    mlp_norm = low(normalize(second_sum, gains[3], shifts[3]))
    hidden_pre = low_back(product(mlp_norm, inner_w) + inner_b)
    activated = low(jax.nn.gelu(hidden_pre))
    return second_sum + low_back(product(activated, outer_w) + outer_b)

def reference(tokens, lengths, latents, norm_gain, norm_bias, cross_qkv, cross_out, self_qkv, self_out, mlp_in, mlp_biases, mlp_out, cotangent):
    half_groups = GROUPS // 2
    counts = jnp.concatenate([lengths[:half_groups, 0], lengths[half_groups:, 1]]).astype(jnp.int32)
    floats = tuple((entry.astype(jnp.float32) for entry in (tokens, latents, norm_gain, norm_bias, cross_qkv, cross_out, self_qkv, self_out, mlp_in, mlp_biases, mlp_out)))

    def forward(tokens_in, latents_in, gains, shifts, cross_w, cross_o, self_w, self_o, inner_w, both_biases, outer_w):
        leading = tokens_in[:half_groups]
        trailing = tokens_in[half_groups:]
        merged_lead = jnp.concatenate([leading[:, :TOK], low_back(trailing[:, :TOK])], 1)
        merged_trail = jnp.concatenate([low_back(leading[:, TOK:]), trailing[:, TOK:]], 1)
        merged = jnp.concatenate([merged_lead, merged_trail], 0)

        def per_group(packed):
            rows_in, count_in = packed
            usable = jnp.arange(2 * TOK) < count_in
            return block_layer(rows_in, usable, latents_in, gains, shifts, cross_w, cross_o, self_w, self_o, inner_w, both_biases, outer_w)
        return lax.map(jax.checkpoint(per_group), (merged, counts))
    result, pullback = jax.vjp(forward, *floats)
    grads = pullback(cotangent.astype(jnp.float32))
    return (result.astype(jnp.bfloat16), grads[0], grads[1], grads[2], grads[3], grads[4], grads[5], grads[6], grads[7], grads[8], grads[9], grads[10])
```

```python
import functools

import jax
import jax.numpy as jnp
from jax import lax
from jax.experimental import pallas as pl
from jax.experimental.pallas import tpu as pltpu
from jax.sharding import PartitionSpec as P

HEADS = 8
BF = jnp.bfloat16
F32 = jnp.float32
MIB = 1 << 20
AXES = ("wide", "narrow")


def dims(contract_left, contract_right):
    return (((contract_left,), (contract_right,)), ((), ()))


def dot(left, right):
    return lax.dot_general(left, right, dims(1, 0), preferred_element_type=F32)


def dot_nt(left, right):
    return lax.dot_general(left, right, dims(1, 1), preferred_element_type=F32)


def dot_tn(left, right):
    return lax.dot_general(left, right, dims(0, 0), preferred_element_type=F32)


def shape(sizes, kind):
    return jax.ShapeDtypeStruct(sizes, kind)


class Order:
    last = None


def call(body, grid, in_specs, out_specs, out_shape, scratch=(), prefetch=0, flops=0, moved=0, limit=60):
    def run(*args):
        specs, first = list(in_specs), prefetch + len(in_specs)
        kernel = body
        if Order.last is not None:
            specs.append(pl.BlockSpec(memory_space=pl.ANY))
            args = (*args, Order.last)

            def kernel(*refs):
                body(*refs[:first], *refs[first + 1 :])

        out = pl.pallas_call(
            kernel,
            grid_spec=pltpu.PrefetchScalarGridSpec(
                num_scalar_prefetch=prefetch,
                grid=grid,
                in_specs=specs,
                out_specs=out_specs,
                scratch_shapes=scratch,
            ),
            out_shape=out_shape,
            compiler_params=pltpu.CompilerParams(vmem_limit_bytes=limit * MIB),
            cost_estimate=pl.CostEstimate(flops=flops, bytes_accessed=moved, transcendentals=0),
        )(*args)
        Order.last = out[0] if isinstance(out, (list, tuple)) else out
        return out

    return run


def whole(sizes):
    return pl.BlockSpec(sizes, lambda *_: (0,) * len(sizes))


CHUNK = 32


def store(ref, at, value):
    ref[at, :] = value


def norm_rows(height, read, write, gain_ref, shift_ref):
    gain, shift = gain_ref[...], shift_ref[...]

    @pl.loop(0, height // CHUNK)
    def _(step):
        place = pl.ds(pl.multiple_of(step * CHUNK, CHUNK), CHUNK)
        write(place, norm(read(place), gain, shift).astype(BF))


def norm_back_rows(height, read, upstream, write, gain_ref, gterm_ref, bterm_ref):
    gain = gain_ref[...]
    width = gain.shape[-1]

    def one(step, sums):
        place = pl.ds(pl.multiple_of(step * CHUNK, CHUNK), CHUNK)
        xhat, scale = norm_stats(read(place))
        above = upstream(place)
        scaled = above * gain
        first = jnp.mean(scaled, -1, keepdims=True)
        second = jnp.mean(scaled * xhat, -1, keepdims=True)
        write(place, scale * (scaled - first - xhat * second))
        fold = lambda value: jnp.sum(value.reshape(CHUNK // 8, 8, width), 0)
        return sums[0] + fold(above * xhat), sums[1] + fold(above)

    none = jnp.zeros((8, width), F32)
    gterm, bterm = lax.fori_loop(0, height // CHUNK, one, (none, none))
    gterm_ref[...] = jnp.sum(gterm, 0, keepdims=True)
    bterm_ref[...] = jnp.sum(bterm, 0, keepdims=True)


def norm_stats(rows):
    mean = jnp.mean(rows, -1, keepdims=True)
    center = rows - mean
    scale = lax.rsqrt(jnp.mean(center * center, -1, keepdims=True) + 1e-05)
    return center * scale, scale


def norm(rows, gain, shift):
    xhat, _ = norm_stats(rows)
    return xhat * gain + shift


def project(rows, gain, shift, weights, first, count, tile=1024):
    height, width = rows.shape
    tiles = width // tile

    def body(rows_ref, gain_ref, shift_ref, weight_ref, low_ref, out_ref):
        @pl.when(pl.program_id(0) == 0)
        def _():
            norm_rows(height, lambda at: rows_ref[at, :].astype(F32), lambda at, v: store(low_ref, at, v), gain_ref, shift_ref)

        out_ref[...] = dot(low_ref[...], weight_ref[...]).astype(BF)

    return call(
        body,
        (count * tiles,),
        [
            whole((height, width)),
            whole((1, width)),
            whole((1, width)),
            pl.BlockSpec((None, width, tile), lambda j: (first + j // tiles, 0, j % tiles)),
        ],
        [
            whole((height, width)),
            pl.BlockSpec((None, height, tile), lambda j: (j // tiles, 0, j % tiles)),
        ],
        [shape((height, width), BF), shape((count, height, width), BF)],
        flops=2 * count * height * width * width,
        moved=2 * (count * width * width + (2 + count) * height * width),
    )(rows, gain, shift, weights)


def attend(limits, queries, pairs, masked):
    array, lead = queries
    _, height, width = array.shape
    size = width // HEADS
    factor = size**-0.5
    chunk = 256

    def body(limit_ref, q_ref, *refs):
        key_refs, value_refs = refs[: len(pairs)], refs[len(pairs) : 2 * len(pairs)]
        mix_ref, total_ref = refs[2 * len(pairs) :]
        for start in range(0, height, chunk):
            query = q_ref[start : start + chunk, :]
            scores = []
            for index, key_ref in enumerate(key_refs):
                score = dot_nt(query, key_ref[...]) * factor
                if masked:
                    place = lax.broadcasted_iota(jnp.int32, score.shape, 1)
                    score = jnp.where(place < limit_ref[index], score, -1000000000.0)
                scores.append(score)
            highest = functools.reduce(jnp.maximum, [jnp.max(s, -1, keepdims=True) for s in scores])
            powers = [jnp.exp(s - highest) for s in scores]
            total = sum(jnp.sum(p, -1, keepdims=True) for p in powers)
            mixed = sum(dot(p.astype(BF), v[...]) for p, v in zip(powers, value_refs))
            mix_ref[start : start + chunk, :] = (mixed / total).astype(BF)
            logged = jnp.broadcast_to(highest + jnp.log(total), (chunk, 128))
            total_ref[:, start : start + chunk] = jnp.transpose(logged)[0:1, :]

    specs = [pl.BlockSpec((None, height, size), lambda h, _: (lead, 0, h))]
    args = [array]
    for place in (1, 2):
        for pair in pairs:
            source, at = pair[0], pair[place]
            specs.append(pl.BlockSpec((None, source.shape[1], size), functools.partial(lambda at, h, _: (at, 0, h), at)))
            args.append(source)
    keys_total = sum(p[0].shape[1] for p in pairs)
    return call(
        body,
        (HEADS,),
        specs,
        [pl.BlockSpec((height, size), lambda h, _: (0, h)), pl.BlockSpec((None, 1, height), lambda h, _: (h, 0, 0))],
        [shape((height, width), BF), shape((HEADS, 1, height), F32)],
        prefetch=1,
        flops=8 * height * keys_total * width,
        moved=4 * (height + keys_total) * width,
    )(limits, *args)


def mix_project(mix, out_weight, base, gain, shift, weights, tile=1024):
    height, width = mix.shape
    count = weights.shape[0]
    tiles = width // tile

    def body(mix_ref, ow_ref, base_ref, gain_ref, shift_ref, weight_ref, total_ref, low_ref, out_ref):
        @pl.when(pl.program_id(0) == 0)
        def _():
            total = base_ref[...].astype(F32) + dot(mix_ref[...], ow_ref[...])
            total_ref[...] = total
            norm_rows(height, lambda at: total_ref[at, :], lambda at, v: store(low_ref, at, v), gain_ref, shift_ref)

        out_ref[...] = dot(low_ref[...], weight_ref[...]).astype(BF)

    return call(
        body,
        (count * tiles,),
        [
            whole((height, width)),
            whole((width, width)),
            whole((height, width)),
            whole((1, width)),
            whole((1, width)),
            pl.BlockSpec((None, width, tile), lambda j: (j // tiles, 0, j % tiles)),
        ],
        [
            whole((height, width)),
            whole((height, width)),
            pl.BlockSpec((None, height, tile), lambda j: (j // tiles, 0, j % tiles)),
        ],
        [shape((height, width), F32), shape((height, width), BF), shape((count, height, width), BF)],
        flops=2 * (count + 1) * height * width * width,
        moved=2 * ((count + 1) * width * width + (6 + count) * height * width),
    )(mix, out_weight, base, gain, shift, weights)


def expand_grad(grad_out, out_weight, tile=1024):
    height, width = grad_out.shape
    hidden = out_weight.shape[0]

    def body(grad_ref, weight_ref, out_ref, sum_ref):
        @pl.when(pl.program_id(0) == 0)
        def _():
            sum_ref[...] = jnp.sum(grad_ref[...].astype(F32), 0, keepdims=True)

        out_ref[...] = dot_nt(grad_ref[...], weight_ref[...]).astype(BF)

    return call(
        body,
        (hidden // tile,),
        [whole((height, width)), pl.BlockSpec((tile, width), lambda j: (j, 0))],
        [pl.BlockSpec((height, tile), lambda j: (0, j)), whole((1, width))],
        [shape((height, hidden), BF), shape((1, width), F32)],
        flops=2 * height * width * hidden,
        moved=2 * (height * width + width * hidden + height * hidden),
    )(grad_out, out_weight)


def mlp_hidden(mix, out_weight, base, gain, shift, in_weight, bias, grad_act, tile=512):
    height, width = mix.shape
    hidden = in_weight.shape[1]
    root = (2.0 / jnp.pi) ** 0.5
    chunk = 256

    def body(mix_ref, ow_ref, base_ref, gain_ref, shift_ref, weight_ref, bias_ref, ga_ref, total_ref, low_ref, act_ref, grad_ref, sum_ref):
        @pl.when(pl.program_id(0) == 0)
        def _():
            total = base_ref[...] + dot(mix_ref[...], ow_ref[...])
            total_ref[...] = total
            norm_rows(height, lambda at: total_ref[at, :], lambda at, v: store(low_ref, at, v), gain_ref, shift_ref)

        sums = jnp.zeros((1, tile), F32)
        for start in range(0, height, chunk):
            rows = slice(start, start + chunk)
            pre = dot(low_ref[rows, :], weight_ref[...]) + bias_ref[...]
            square = pre * pre
            bent = jnp.tanh(pre * (root + (root * 0.044715) * square))
            half = 0.5 + 0.5 * bent
            act_ref[rows, :] = (pre * half).astype(BF)
            slope = half + (0.5 * pre) * (1.0 - bent * bent) * (root + (3 * root * 0.044715) * square)
            grad = (ga_ref[rows, :].astype(F32) * slope).astype(BF)
            grad_ref[rows, :] = grad
            sums += jnp.sum(grad.astype(F32), 0, keepdims=True)
        sum_ref[...] = sums

    return call(
        body,
        (hidden // tile,),
        [
            whole((height, width)),
            whole((width, width)),
            whole((height, width)),
            whole((1, width)),
            whole((1, width)),
            pl.BlockSpec((width, tile), lambda j: (0, j)),
            pl.BlockSpec((1, tile), lambda j: (0, j)),
            pl.BlockSpec((height, tile), lambda j: (0, j)),
        ],
        [
            whole((height, width)),
            whole((height, width)),
            pl.BlockSpec((height, tile), lambda j: (0, j)),
            pl.BlockSpec((height, tile), lambda j: (0, j)),
            pl.BlockSpec((1, tile), lambda j: (0, j)),
        ],
        [
            shape((height, width), F32),
            shape((height, width), BF),
            shape((height, hidden), BF),
            shape((height, hidden), BF),
            shape((1, hidden), F32),
        ],
        flops=2 * height * width * (width + hidden),
        moved=2 * (width * width + width * hidden + 3 * height * hidden + 6 * height * width),
    )(mix, out_weight, base, gain, shift, in_weight, bias, grad_act)


def mlp_result(active, out_weight, bias, base, tile=512):
    height, hidden = active.shape
    width = out_weight.shape[1]

    def body(act_ref, weight_ref, bias_ref, base_ref, out_ref):
        out_ref[...] = (base_ref[...] + (dot(act_ref[...], weight_ref[...]) + bias_ref[...])).astype(BF)

    return call(
        body,
        (width // tile,),
        [
            whole((height, hidden)),
            pl.BlockSpec((hidden, tile), lambda j: (0, j)),
            pl.BlockSpec((1, tile), lambda j: (0, j)),
            pl.BlockSpec((height, tile), lambda j: (0, j)),
        ],
        pl.BlockSpec((height, tile), lambda j: (0, j)),
        shape((height, width), BF),
        flops=2 * height * width * hidden,
        moved=2 * (hidden * width + height * hidden + 3 * height * width),
    )(active, out_weight, bias, base)


def second_grad(hidden_grad, in_weight, grad_out, second, gain, out_weight, tile=1024):
    height, hidden = hidden_grad.shape
    width = in_weight.shape[0]
    steps = hidden // tile

    def body(hg_ref, weight_ref, go_ref, second_ref, gain_ref, ow_ref, full_ref, low_ref, mix_ref, gterm_ref, bterm_ref, total):
        part = dot_nt(hg_ref[...], weight_ref[...])
        step = pl.program_id(0)

        @pl.when(step == 0)
        def _():
            total[...] = part

        @pl.when(step > 0)
        def _():
            total[...] += part

        @pl.when(step == steps - 1)
        def _():
            def write(at, grad):
                grad = grad + go_ref[at, :].astype(F32)
                full_ref[at, :] = grad
                low_ref[at, :] = grad.astype(BF)

            norm_back_rows(height, lambda at: second_ref[at, :], lambda at: total[at, :], write, gain_ref, gterm_ref, bterm_ref)
            mix_ref[...] = dot_nt(low_ref[...], ow_ref[...]).astype(BF)

    return call(
        body,
        (steps,),
        [
            pl.BlockSpec((height, tile), lambda j: (0, j)),
            pl.BlockSpec((width, tile), lambda j: (0, j)),
            whole((height, width)),
            whole((height, width)),
            whole((1, width)),
            whole((width, width)),
        ],
        [whole((height, width))] * 3 + [whole((1, width))] * 2,
        [shape((height, width), F32), shape((height, width), BF), shape((height, width), BF)] + [shape((1, width), F32)] * 2,
        scratch=[pltpu.VMEM((height, width), F32)],
        flops=2 * height * width * (width + hidden),
        moved=2 * (width * width + width * hidden + height * hidden + 7 * height * width),
    )(hidden_grad, in_weight, grad_out, second, gain, out_weight)


def attend_back(limits, queries, pairs, totals, grad_mix, masked):
    array, lead = queries
    _, height, width = array.shape
    size = width // HEADS
    factor = size**-0.5
    chunk = 256
    count = len(pairs)

    def body(limit_ref, q_ref, total_ref, grad_ref, *refs):
        key_refs, value_refs = refs[:count], refs[count : 2 * count]
        dq_ref, pair_refs, sums = refs[2 * count], refs[2 * count + 1 : 3 * count + 1], refs[3 * count + 1 :]
        for start in range(0, height, chunk):
            rows = slice(start, start + chunk)
            query, grad = q_ref[rows, :], grad_ref[rows, :]
            logged = total_ref[:, rows]
            probs, slopes = [], []
            for index in range(count):
                score = dot_nt(key_refs[index][...], query) * factor
                if masked:
                    place = lax.broadcasted_iota(jnp.int32, score.shape, 0)
                    score = jnp.where(place < limit_ref[index], score, -1000000000.0)
                probs.append(jnp.exp(score - logged))
                slopes.append(dot_nt(value_refs[index][...], grad))
            delta = sum(jnp.sum(p * s, 0, keepdims=True) for p, s in zip(probs, slopes))
            dq = None
            for index in range(count):
                dv = dot(probs[index].astype(BF), grad)
                ds = (probs[index] * (slopes[index] - delta)).astype(BF)
                dk = dot(ds, query)
                part = dot_tn(ds, key_refs[index][...])
                dq = part if dq is None else dq + part
                acc = sums[index]
                if start == 0:
                    acc[0] = dk
                    acc[1] = dv
                else:
                    acc[0] += dk
                    acc[1] += dv
            dq_ref[rows, :] = (dq * factor).astype(BF)
        for index in range(count):
            pair_refs[index][0] = (sums[index][0] * factor).astype(BF)
            pair_refs[index][1] = sums[index][1].astype(BF)

    specs = [
        pl.BlockSpec((None, height, size), lambda h, _: (lead, 0, h)),
        pl.BlockSpec((None, 1, height), lambda h, _: (h, 0, 0)),
        pl.BlockSpec((height, size), lambda h, _: (0, h)),
    ]
    args = [array, totals, grad_mix]
    for place in (1, 2):
        for pair in pairs:
            source, at = pair[0], pair[place]
            specs.append(pl.BlockSpec((None, source.shape[1], size), functools.partial(lambda at, h, _: (at, 0, h), at)))
            args.append(source)
    heights = [p[0].shape[1] for p in pairs]
    return call(
        body,
        (HEADS,),
        specs,
        [pl.BlockSpec((height, size), lambda h, _: (0, h))]
        + [pl.BlockSpec((2, keys, size), lambda h, _: (0, 0, h)) for keys in heights],
        [shape((height, width), BF)] + [shape((2, keys, width), BF) for keys in heights],
        scratch=[pltpu.VMEM((2, keys, size), F32) for keys in heights],
        prefetch=1,
        flops=20 * height * sum(heights) * width,
        moved=8 * (height + sum(heights)) * width,
    )(limits, *args)


def norm_grad(sources, rows, gain, extra, out_weight, kind, tile=1024):
    height, width = rows.shape
    count = len(sources)
    tiles = width // tile
    has_extra, has_out = extra is not None, out_weight is not None

    def body(*refs):
        refs = list(refs)
        source_refs, weight_refs = refs[:count], refs[count : 2 * count]
        rest = refs[2 * count :]
        rows_ref, gain_ref = rest[:2]
        rest = rest[2:]
        extra_ref = rest.pop(0) if has_extra else None
        ow_ref = rest.pop(0) if has_out else None
        grad_ref = rest.pop(0)
        mix_ref = rest.pop(0) if has_out else None
        gterm_ref, bterm_ref, total = rest
        step = pl.program_id(0)
        part = None
        for source_ref, weight_ref in zip(source_refs, weight_refs):
            piece = dot_nt(source_ref[...], weight_ref[...])
            part = piece if part is None else part + piece

        @pl.when(step == 0)
        def _():
            total[...] = part

        @pl.when(step > 0)
        def _():
            total[...] += part

        @pl.when(step == tiles - 1)
        def _():
            def write(at, grad):
                if has_extra:
                    grad = grad + extra_ref[at, :].astype(F32)
                grad_ref[at, :] = grad.astype(kind)

            norm_back_rows(
                height, lambda at: rows_ref[at, :].astype(F32), lambda at: total[at, :], write, gain_ref, gterm_ref, bterm_ref
            )
            if has_out:
                mix_ref[...] = dot_nt(grad_ref[...], ow_ref[...]).astype(BF)

    specs, args = [], []
    for array, lead, _, _ in sources:
        if lead is None:
            specs.append(pl.BlockSpec((height, tile), lambda j: (0, j)))
        else:
            specs.append(pl.BlockSpec((None, height, tile), functools.partial(lambda lead, j: (lead, 0, j), lead)))
        args.append(array)
    for _, _, weights, at in sources:
        specs.append(pl.BlockSpec((None, width, tile), functools.partial(lambda at, j: (at, 0, j), at)))
        args.append(weights)
    specs += [whole((height, width)), whole((1, width))]
    args += [rows, gain]
    if has_extra:
        specs.append(whole((height, width)))
        args.append(extra)
    if has_out:
        specs.append(whole((width, width)))
        args.append(out_weight)
    outs = [shape((height, width), kind)] + ([shape((height, width), BF)] if has_out else [])
    return call(
        body,
        (tiles,),
        specs,
        [whole((height, width))] * len(outs) + [whole((1, width))] * 2,
        outs + [shape((1, width), F32)] * 2,
        scratch=[pltpu.VMEM((height, width), F32)],
        flops=2 * height * width * width * (count + has_out),
        moved=2 * ((count + has_out) * width * width + (count + 5) * height * width),
    )(*args)


BITS = {"core": ("narrow", 0), "x": ("narrow", 1), "y": ("wide", 0), "z": ("wide", 1), "zz": ("wide", 2)}


def grad_blocks(place, items, order, flip, received):
    specs, args, plans, row, scratch, flops = [], [], [], 0, [], 0

    def add(array, lead, block, split):
        def index(j, place_ref):
            narrow = place_ref[0] ^ (2 * j + flip)
            at = (narrow if split == 0 else 0, narrow if split == 1 else 0)
            return at if lead is None else (lead, *at)

        specs.append(pl.BlockSpec(block if lead is None else (None, *block), index))
        args.append(array)

    for item in items:
        if item[0] == "outer":
            lefts, rights = item[1], item[2]
            rows = lefts[0][0].shape[-1] // 4
            cols = rights[0][0].shape[-1] // 8
            for array, lead in lefts:
                add(array, lead, (array.shape[-2], rows), 1)
            for array, lead in rights:
                add(array, lead, (array.shape[-2], 8 * cols), None)
                if cols < 256:
                    scratch.append(pltpu.VMEM((array.shape[-2], 8 * cols), BF))
            plans.append(("outer", len(lefts), rows, cols, row))
            row += rows * cols // 128
            flops += sum(2 * a.shape[-2] * rows * 2 * cols * 8 for a, _ in lefts)
        elif item[0] == "rows":
            rows = item[1].shape[0] // 4
            add(item[1], None, (rows, item[1].shape[1]), 0)
            plans.append(("rows", 1, rows, 128, row))
            row += rows
        else:
            array = item[1]
            rows = array.shape[2]
            specs.append(pl.BlockSpec((None, 8, rows, 128), lambda j, place_ref: (place_ref[0] ^ (2 * j + flip), 0, 0, 0)))
            args.append(array)
            plans.append(("ready", 1, rows, 128, row))
            row += rows
    later = order[1:]
    out_spec = pl.BlockSpec(
        tuple(None if bit == "x" else 2 for bit in later) + (row, 128),
        lambda j, place_ref: tuple(j if bit == "x" else 0 for bit in later) + (0, 0),
    )
    halves = [out_spec, out_spec]
    if received is not None:
        specs += halves
        args += received
    n_in = len(args)

    def body(place_ref, *refs):
        outs = refs[n_in : n_in + 2]
        got = refs[n_in - 2 : n_in] if received is not None else None
        turned = list(refs[n_in + 2 :])
        wide_me = place_ref[1]
        step = pl.program_id(0)

        def fill(side):
            def put(away, first, value):
                index = tuple((away >> BITS[bit][1]) & 1 for bit in later if bit != "x")
                half = side if side is not None else (away >> BITS[order[0]][1]) & 1
                at = (*index, slice(first, first + value.shape[0]), slice(None))
                if got is not None:
                    value = value + got[half][at].astype(F32)
                outs[half][at] = value.astype(BF)

            at, spare = 0, 0
            for kind, count, rows, cols, first in plans:
                if kind == "outer":
                    lefts, rights = refs[at : at + count], refs[at + count : at + 2 * count]
                    at += 2 * count
                    if cols < 256:
                        sorted_refs = turned[spare : spare + count]
                        spare += count
                        tile = min(rows, 512)
                        for top in range(0, rows, tile):
                            product = sum(dot_tn(a[:, top : top + tile], b[...]) for a, b in zip(lefts, sorted_refs))
                            for away in range(8):
                                put(away, first + top, product[:, away * cols : away * cols + cols])
                    else:
                        for away in range(8):
                            columns = pl.ds(pl.multiple_of((wide_me ^ away) * cols, cols), cols)
                            product = sum(dot_tn(a[...], b[:, columns]) for a, b in zip(lefts, rights))
                            for part in range(cols // 128):
                                put(away, first + part * rows, product[:, part * 128 : part * 128 + 128])
                elif kind == "rows":
                    ref = refs[at]
                    at += 1
                    for away in range(8):
                        columns = pl.ds(pl.multiple_of((wide_me ^ away) * 128, 128), 128)
                        put(away, first, ref[:, columns].astype(F32))
                else:
                    ref = refs[at]
                    at += 1
                    for away in range(8):
                        put(away, first, ref[wide_me ^ away].astype(F32))

        @pl.when(step == 0)
        def _():
            at, spare = 0, 0
            for kind, count, rows, cols, first in plans:
                rights = refs[at + count : at + 2 * count]
                at += 2 * count if kind == "outer" else 1
                if kind == "outer" and cols < 256:
                    for ref in rights:
                        for away in range(8):
                            columns = pl.ds(pl.multiple_of((wide_me ^ away) * cols, cols), cols)
                            turned[spare][:, away * cols : away * cols + cols] = ref[:, columns]
                        spare += 1

        if order[0] == "x":
            for side in range(2):
                pl.when(step == side)(functools.partial(fill, side))
        else:
            fill(None)

    return call(
        body,
        (2,),
        specs,
        halves,
        [shape((2, 2, 2, row, 128), BF)] * 2,
        scratch=scratch,
        prefetch=1,
        flops=flops,
        moved=2 * 16 * row * 128 * (2 if received is not None else 1) + sum(2 * a.size for a in args),
    )(place, *args)


def swap(value, bit):
    axis, index = BITS[bit]
    pairs = [(source, source ^ (1 << index)) for source in range(lax.axis_size(axis))]
    return lax.ppermute(value, axis, pairs)


def total_of(parts):
    return sum(part.astype(F32) for part in parts)


class Reduction:
    def __init__(self, place, items, order):
        self.place, self.items, self.order = place, items, order

    def send(self):
        sent = grad_blocks(self.place, self.items, self.order, 1, None)
        self.arrived = [swap(half, "core") for half in sent]
        return self

    def keep(self):
        kept, sent = grad_blocks(self.place, self.items, self.order, 0, self.arrived)
        self.parts = [kept, swap(sent, self.order[0])]
        return self

    def finish(self):
        parts = self.parts
        for bit in self.order[1:]:
            arrived = swap(total_of([part[1] for part in parts]).astype(BF), bit)
            parts = [part[0] for part in parts] + [arrived]
        return total_of(parts)


def outer_sum(lefts, rights):
    return sum(lax.dot_general(a, b, dims(0, 0), preferred_element_type=F32) for a, b in zip(lefts, rights))


def to_blocks(term, wide_count, narrow_count):
    lead, rows, cols = term.shape
    split = term.reshape(lead, narrow_count, rows // narrow_count, wide_count, cols // wide_count)
    moved = jnp.transpose(split, (3, 1, 0, 2, 4))
    return moved.reshape(wide_count * narrow_count, lead, rows // narrow_count, cols // wide_count)


def from_partner(value, axis, bit):
    mask = 2**bit
    pairs = [(source, source ^ mask) for source in range(lax.axis_size(axis))]
    return lax.ppermute(value, axis, pairs)


def on_device(
    tokens,
    lengths,
    latents,
    norm_gain,
    norm_bias,
    cross_qkv,
    cross_out,
    self_qkv,
    self_out,
    mlp_in,
    mlp_biases,
    mlp_out,
    cotangent,
):
    Order.last = None
    half_rows = tokens.shape[1] // 2
    width = tokens.shape[2]
    hidden_width = mlp_in.shape[1]
    wide_size = lax.axis_size("wide")
    narrow_size = lax.axis_size("narrow")
    wide_me = lax.axis_index("wide")
    narrow_me = lax.axis_index("narrow")
    place = jnp.stack([narrow_me, wide_me]).astype(jnp.int32)
    leader = wide_me < wide_size // 2
    partner_bit = wide_size.bit_length() - 2
    own_rows = tokens[0]
    outgoing = lax.dynamic_slice(own_rows, (jnp.where(leader, half_rows, 0), 0), (half_rows, width))
    incoming = from_partner(outgoing, "wide", partner_bit)
    kept = lax.dynamic_slice(own_rows, (jnp.where(leader, 0, half_rows), 0), (half_rows, width))
    length = jnp.where(leader, lengths[0, 0], lengths[0, 1])
    limits = jnp.stack([jnp.where(leader, length, length - half_rows), jnp.where(leader, length - half_rows, length)])
    gains = [norm_gain[i : i + 1] for i in range(4)]
    shifts = [norm_bias[i : i + 1] for i in range(4)]
    inner_bias = mlp_biases[None, :hidden_width]
    outer_bias = mlp_biases[None, hidden_width:]
    grad_out = cotangent[0]

    latent_low, query = project(latents, gains[1], shifts[1], cross_qkv, 0, 1)
    kept_low, kept_kv = project(kept, gains[0], shifts[0], cross_qkv, 1, 2)
    grad_act, grad_out_bias = expand_grad(grad_out, mlp_out)
    other_low, other_kv = project(incoming, gains[0], shifts[0], cross_qkv, 1, 2)
    pairs = [(kept_kv, 0, 1), (other_kv, 0, 1)]
    cross_mix, cross_total = attend(limits, (query, 0), pairs, True)
    first_sum, self_low, self_q = mix_project(cross_mix, cross_out, latents, gains[2], shifts[2], self_qkv)
    self_pairs = [(self_q, 1, 2)]
    self_mix, self_total = attend(limits, (self_q, 0), self_pairs, False)
    second_sum, mlp_low, active, hidden_low, grad_mlp_bias = mlp_hidden(
        self_mix, self_out, first_sum, gains[3], shifts[3], mlp_in, inner_bias, grad_act
    )
    fast = (narrow_size, wide_size) == (4, 8)
    mlp_out_items = [("outer", [(active, None)], [(grad_out, None)])]
    mlp_in_items = [("outer", [(mlp_low, None)], [(hidden_low, None)])]
    if fast:
        sums_out = Reduction(place, mlp_out_items, ("x", "y", "z", "zz")).send()
        sums_in = Reduction(place, mlp_in_items, ("y", "x", "z", "zz")).send()
        sums_out.keep()
        sums_in.keep()
    grad_second, second_low, grad_self_mix, gain_mlp, shift_mlp = second_grad(
        hidden_low, mlp_in, grad_out, second_sum, gains[3], self_out
    )
    self_gq, self_gkv = attend_back(limits, (self_q, 0), self_pairs, self_total, grad_self_mix, False)
    self_items = [
        ("outer", [(self_mix, None)], [(second_low, None)]),
        ("outer", [(self_low, None)], [(self_gq, None)]),
        ("outer", [(self_low, None)], [(self_gkv, 0)]),
        ("outer", [(self_low, None)], [(self_gkv, 1)]),
    ]
    if fast:
        sums_self = Reduction(place, self_items, ("z", "x", "y", "zz")).send().keep()
    first_low, grad_cross_mix, gain_self, shift_self = norm_grad(
        [(self_gq, None, self_qkv, 0), (self_gkv, 0, self_qkv, 1), (self_gkv, 1, self_qkv, 2)],
        first_sum,
        gains[2],
        grad_second,
        cross_out,
        BF,
    )
    cross_gq, kept_gkv, other_gkv = attend_back(limits, (query, 0), pairs, cross_total, grad_cross_mix, True)
    back_sent, gain_other, shift_other = norm_grad(
        [(other_gkv, 0, cross_qkv, 1), (other_gkv, 1, cross_qkv, 2)], incoming, gains[0], None, None, BF
    )
    returned = from_partner(back_sent, "wide", partner_bit)
    cross_items = [("outer", [(cross_mix, None)], [(first_low, None)])]
    query_items = [("outer", [(latent_low, None)], [(cross_gq, None)])]
    pair_items = [
        ("outer", [(kept_low, None), (other_low, None)], [(kept_gkv, at), (other_gkv, at)]) for at in range(2)
    ]
    if fast:
        sums_cross = Reduction(place, cross_items + query_items, ("x", "y", "z", "zz")).send()
        sums_pair = Reduction(place, pair_items, ("y", "z", "x", "zz")).send()
        sums_cross.keep()
        sums_pair.keep()
    grad_kept, gain_kept, shift_kept = norm_grad(
        [(kept_gkv, 0, cross_qkv, 1), (kept_gkv, 1, cross_qkv, 2)], kept, gains[0], None, None, F32
    )
    grad_latents, gain_latent, shift_latent = norm_grad(
        [(cross_gq, None, cross_qkv, 0)], latents, gains[1], first_low, None, BF
    )
    gain_terms = jnp.concatenate([gain_kept + gain_other, gain_latent, gain_self, gain_mlp])
    bias_terms = jnp.concatenate([shift_kept + shift_other, shift_latent, shift_self, shift_mlp])
    bias_vector = jnp.concatenate([grad_mlp_bias, grad_out_bias], 1)[0]
    if fast:
        per_bias = bias_vector.size // (wide_size * narrow_size)
        small = jnp.concatenate(
            [
                gain_terms.reshape(4, 8, 1, 128),
                bias_terms.reshape(4, 8, 1, 128),
                jnp.pad(
                    jnp.transpose(bias_vector.reshape(8, 4, per_bias), (1, 0, 2)), ((0, 0), (0, 0), (0, 14 * 128 - per_bias))
                ).reshape(4, 8, 14, 128),
            ],
            2,
        )
        sums_small = Reduction(place, [("rows", grad_latents), ("ready", small)], ("z", "x", "y", "zz")).send().keep()
        result = mlp_result(active, mlp_out, outer_bias, second_sum)
        outs_out, outs_in, outs_self, outs_cross, outs_pair, outs_small = [
            sums.finish() for sums in (sums_out, sums_in, sums_self, sums_cross, sums_pair, sums_small)
        ]
        rows = width // 4
        deep = rows
        shares = (
            outs_small[: grad_latents.shape[0] // 4],
            outs_small[-16:-15],
            outs_small[-15:-14],
            jnp.concatenate([outs_cross[deep:][None], outs_pair.reshape(2, rows, 128)]),
            outs_cross[:deep],
            outs_self[rows:].reshape(3, rows, 128),
            outs_self[:rows],
            jnp.transpose(outs_in.reshape(-1, rows, 128), (1, 0, 2)).reshape(rows, -1),
            outs_small[-14:].reshape(-1)[:per_bias],
            outs_out,
        )
    else:
        result = mlp_result(active, mlp_out, outer_bias, second_sum)

        def outer(item):
            pick = lambda entry: entry[0] if entry[1] is None else entry[0][entry[1]]
            return outer_sum([pick(e) for e in item[1]], [pick(e) for e in item[2]])

        matrices = (
            grad_latents.astype(F32)[None],
            gain_terms[None],
            bias_terms[None],
            jnp.stack([outer(item) for item in query_items + pair_items]),
            outer(cross_items[0])[None],
            jnp.stack([outer(item) for item in self_items[1:]]),
            outer(self_items[0])[None],
            outer(mlp_in_items[0])[None],
            outer(mlp_out_items[0])[None],
        )
        blocked = tuple(to_blocks(term, wide_size, narrow_size) for term in matrices) + (
            bias_vector.reshape(wide_size * narrow_size, 1, 1, -1),
        )
        summed = lax.psum_scatter(blocked, AXES, scatter_dimension=0, tiled=True)
        s = tuple(entry[0] for entry in summed)
        shares = (s[0][0], s[1][0], s[2][0], s[3], s[4][0], s[5], s[6][0], s[7][0], s[9].reshape(-1), s[8][0])
    returned = returned.astype(F32)
    tokens_grad = jnp.where(
        leader, jnp.concatenate([grad_kept, returned]), jnp.concatenate([returned, grad_kept])
    )
    return (result[None], tokens_grad[None], *shares)


def solution(mesh):
    return jax.shard_map(
        on_device,
        mesh=mesh,
        in_specs=(
            P(("wide", "narrow"), None, None),
            P(("wide", "narrow"), None),
            P(),
            P(),
            P(),
            P(),
            P(),
            P(),
            P(),
            P(),
            P(),
            P(),
            P(("wide", "narrow"), None, None),
        ),
        out_specs=(
            P(("wide", "narrow"), None, None),
            P(("wide", "narrow"), None, None),
            P("narrow", "wide"),
            P("narrow", "wide"),
            P("narrow", "wide"),
            P(None, "narrow", "wide"),
            P("narrow", "wide"),
            P(None, "narrow", "wide"),
            P("narrow", "wide"),
            P("narrow", "wide"),
            P(("wide", "narrow")),
            P("narrow", "wide"),
        ),
        check_vma=False,
    )
```

```python
import functools

import jax
import jax.numpy as jnp
from jax import lax
from jax.experimental import pallas as pl
from jax.experimental.pallas import tpu as pltpu
from jax.sharding import PartitionSpec as P

HEADS = 8
BF = jnp.bfloat16
F32 = jnp.float32
MIB = 1 << 20
LOG2E = 1.4426950408889634
AXES = ("wide", "narrow")


def dims(contract_left, contract_right):
    return (((contract_left,), (contract_right,)), ((), ()))


def dot(left, right):
    return lax.dot_general(left, right, dims(1, 0), preferred_element_type=F32)


def dot_nt(left, right):
    return lax.dot_general(left, right, dims(1, 1), preferred_element_type=F32)


def dot_tn(left, right):
    return lax.dot_general(left, right, dims(0, 0), preferred_element_type=F32)


def shape(sizes, kind):
    return jax.ShapeDtypeStruct(sizes, kind)


class Order:
    last = []
    token = None


def call(body, out_shape, scratch=(), scalars=0, flops=0, limit=16, outs_far=False, last_far=0, name=None):
    def run(*args):
        count, single = len(args), not isinstance(out_shape, (list, tuple))
        shapes = [out_shape] if single else list(out_shape)
        n_out = len(shapes)
        specs = [pl.BlockSpec(memory_space=pltpu.SMEM)] * scalars + [pl.BlockSpec(memory_space=pltpu.VMEM)] * (count - scalars)
        for index in range(count - last_far, count):
            specs[index] = pl.BlockSpec(memory_space=pl.ANY)
        specs += [pl.BlockSpec(memory_space=pl.ANY) for _ in Order.last]
        after = count + len(Order.last)
        if outs_far:
            shapes = [pltpu.HBM(entry.shape, entry.dtype) for entry in shapes]

        def kernel(*refs):
            refs[after + n_out][...] = jnp.zeros((8, 128), F32)
            body(*refs[:count], *refs[after : after + n_out], *refs[after + n_out + 1 :])

        *out, token = pl.pallas_call(
            kernel,
            in_specs=specs,
            out_specs=[pl.BlockSpec(memory_space=pl.ANY if outs_far else pltpu.VMEM)] * n_out
            + [pl.BlockSpec(memory_space=pltpu.VMEM)],
            scratch_shapes=scratch,
            out_shape=shapes + [pltpu.VMEM((8, 128), F32)],
            name=name,
            compiler_params=pltpu.CompilerParams(vmem_limit_bytes=limit * MIB),
            cost_estimate=pl.CostEstimate(
                flops=COSTS.get(name, int(flops * COSTS["rest"])), bytes_accessed=0, transcendentals=0
            ),
        )(*args, *Order.last)
        Order.last = [token]
        Order.token = token
        return out[0] if single else out

    return run


def norm_stats(rows):
    mean = jnp.mean(rows, -1, keepdims=True)
    center = rows - mean
    scale = lax.rsqrt(jnp.mean(center * center, -1, keepdims=True) + 1e-05)
    return center * scale, scale


def norm(rows, gain, shift):
    xhat, _ = norm_stats(rows)
    return xhat * gain + shift


def norm_back(rows, gain, upstream):
    xhat, scale = norm_stats(rows)
    scaled = upstream * gain
    first = jnp.mean(scaled, -1, keepdims=True)
    second = jnp.mean(scaled * xhat, -1, keepdims=True)
    return (
        scale * (scaled - first - xhat * second),
        jnp.sum(upstream * xhat, 0, keepdims=True),
        jnp.sum(upstream, 0, keepdims=True),
    )


def pieces(height, size):
    return [slice(start, start + size) for start in range(0, height, size)]


def project(name, rows, gain, shift, weights, first, count):
    height, width = rows.shape

    def body(rows_ref, gain_ref, shift_ref, weight_ref, low_ref, out_ref):
        for at in pieces(height, 256):
            low = norm(rows_ref[at, :].astype(F32), gain_ref[...], shift_ref[...]).astype(BF)
            low_ref[at, :] = low
            for index in range(count):
                out_ref[index, at, :] = dot(low, weight_ref[index]).astype(BF)

    return call(
        body,
        [shape((height, width), BF), shape((count, height, width), BF)],
        name=name,
        flops=2 * count * height * width * width,
    )(rows, gain, shift, weights[first : first + count])


def attend(name, limits, queries, pairs, masked, before=None, last=True):
    array, lead = queries
    _, height, width = array.shape
    size = width // HEADS
    factor = size**-0.5
    count = len(pairs)
    earlier = 0 if before is None else 2

    def body(limit_ref, q_ref, *refs):
        refs, had, outs = refs[:count], refs[count : count + earlier], refs[count + earlier :]
        for head in range(HEADS):
            cols = slice(head * size, head * size + size)
            here = slice(head, head + 1)
            scores = []
            for index, ref in enumerate(refs):
                score = dot_nt(q_ref[lead, :, cols], ref[pairs[index][1], :, cols])
                if masked:
                    place = lax.broadcasted_iota(jnp.int32, score.shape, 1)
                    score = jnp.where(place < limit_ref[index], score, -1e10)
                scores.append(score)
            highest = functools.reduce(jnp.maximum, [jnp.max(s, -1, keepdims=True) for s in scores])
            if had:
                highest = jnp.maximum(jnp.broadcast_to(highest, (height, size)), had[1][0, head])
            over = lambda s: s - (jnp.concatenate([highest] * (s.shape[1] // size), 1) if had else highest)
            powers = [jnp.exp2(over(s) * (factor * LOG2E)) for s in scores]
            total = sum(jnp.sum(p, -1, keepdims=True) for p in powers)
            mixed = sum(dot(p.astype(BF), ref[pair[2], :, cols]) for p, ref, pair in zip(powers, refs, pairs))
            if had:
                share = jnp.exp2((had[1][0, head] - highest) * (factor * LOG2E))
                total = total + share * had[1][1, head]
                mixed = mixed + share * had[0][:, cols]
            if not last:
                outs[0][:, cols] = mixed
                outs[1][0, head] = jnp.broadcast_to(highest, (height, size))
                outs[1][1, head] = jnp.broadcast_to(total, (height, size))
                continue
            mixed = mixed / total
            outs[2][:, cols] = mixed
            outs[0][:, cols] = mixed.astype(BF)
            logged = jnp.broadcast_to(highest * factor + jnp.log(total), (height, size))
            outs[1][here, :] = jnp.transpose(logged)[0:1, :]

    keys_total = sum(p[0].shape[1] for p in pairs)
    if last:
        outs = [shape((height, width), BF), shape((HEADS, height), F32), shape((height, width), F32)]
    else:
        outs = [shape((height, width), F32), shape((2, HEADS, height, size), F32)]
    return call(
        body,
        outs,
        scalars=1,
        name=name,
        flops=8 * height * keys_total * width,
    )(limits, array, *[p[0] for p in pairs], *(before or []))


def mix_project(name, mix, out_weight, base, gain, shift, weights):
    height, width = mix.shape
    count = weights.shape[0]

    def body(mix_ref, ow_ref, base_ref, gain_ref, shift_ref, weight_ref, total_ref, low_ref, out_ref):
        for at in pieces(height, 256):
            total = base_ref[at, :].astype(F32) + dot(mix_ref[at, :], ow_ref[...])
            total_ref[at, :] = total
            low = norm(total, gain_ref[...], shift_ref[...]).astype(BF)
            low_ref[at, :] = low
            for index in range(count):
                out_ref[index, at, :] = dot(low, weight_ref[index]).astype(BF)

    return call(
        body,
        [shape((height, width), F32), shape((height, width), BF), shape((count, height, width), BF)],
        name=name,
        flops=2 * (count + 1) * height * width * width,
    )(mix, out_weight, base, gain, shift, weights)


def expand_grad(name, grad_out, out_weight):
    height, width = grad_out.shape
    hidden = out_weight.shape[0]

    def body(grad_ref, weight_ref, out_ref, sum_ref):
        sum_ref[...] = jnp.sum(grad_ref[...].astype(F32), 0, keepdims=True)
        for at in pieces(hidden, 1024):
            out_ref[:, at] = dot_nt(grad_ref[...], weight_ref[at, :]).astype(BF)

    return call(
        body,
        [shape((height, hidden), BF), shape((1, width), F32)],
        name=name,
        flops=2 * height * width * hidden,
    )(grad_out, out_weight)


def mlp_hidden(name, mix, out_weight, base, gain, shift, in_weight, bias, grad_act):
    height, width = mix.shape
    hidden = in_weight.shape[1]
    root = (2.0 / jnp.pi) ** 0.5
    tile, chunk = 512, 256

    def body(mix_ref, ow_ref, base_ref, gain_ref, shift_ref, weight_ref, bias_ref, ga_ref, total_ref, low_ref, act_ref, grad_ref, sum_ref):
        for at in pieces(height, 256):
            total = base_ref[at, :] + dot(mix_ref[at, :], ow_ref[...])
            total_ref[at, :] = total
            low_ref[at, :] = norm(total, gain_ref[...], shift_ref[...]).astype(BF)

        for cols in pieces(hidden, tile):
            sums = jnp.zeros((8, tile), F32)
            for rows in pieces(height, chunk):
                pre = dot(low_ref[rows, :], weight_ref[:, cols]) + bias_ref[:, cols]
                square = pre * pre
                half = 0.5 + 0.5 * jnp.tanh(pre * (root + (root * 0.044715) * square))
                act_ref[rows, cols] = (pre * half).astype(BF)
                slope = half * (1.0 + (1.0 - half) * (pre * (2 * root + (6 * root * 0.044715) * square)))
                grad = ga_ref[rows, cols].astype(F32) * slope
                grad_ref[rows, cols] = grad.astype(BF)
                sums += jnp.sum(grad.reshape(chunk // 8, 8, tile), 0)
            sum_ref[:, cols] = jnp.sum(sums, 0, keepdims=True)

    return call(
        body,
        [
            shape((height, width), F32),
            shape((height, width), BF),
            shape((height, hidden), BF),
            shape((height, hidden), BF),
            shape((1, hidden), F32),
        ],
        name=name,
        flops=2 * height * width * (width + hidden),
    )(mix, out_weight, base, gain, shift, in_weight, bias, grad_act)


def mlp_result(name, active, out_weight, bias, base):
    height, hidden = active.shape
    width = out_weight.shape[1]

    def body(act_ref, weight_ref, bias_ref, base_ref, out_ref):
        for at in pieces(width, 512):
            out_ref[:, at] = (base_ref[:, at] + (dot(act_ref[...], weight_ref[:, at]) + bias_ref[:, at])).astype(BF)

    return call(
        body,
        shape((height, width), BF),
        name=name,
        flops=2 * height * width * hidden,
    )(active, out_weight, bias, base)


def second_grad(name, hidden_grad, in_weight, grad_out, second, gain, out_weight):
    height, hidden = hidden_grad.shape
    width = in_weight.shape[0]

    def body(hg_ref, weight_ref, go_ref, second_ref, gain_ref, ow_ref, full_ref, low_ref, mix_ref, gterm_ref, bterm_ref):
        gterms, bterms = [], []
        for at in pieces(height, 256):
            upstream = dot_nt(hg_ref[at, :], weight_ref[...])
            grad, gterm, bterm = norm_back(second_ref[at, :], gain_ref[...], upstream)
            gterms.append(gterm)
            bterms.append(bterm)
            grad = grad + go_ref[at, :].astype(F32)
            full_ref[at, :] = grad
            low = grad.astype(BF)
            low_ref[at, :] = low
            mix_ref[at, :] = dot_nt(low, ow_ref[...]).astype(BF)
        gterm_ref[...] = sum(gterms)
        bterm_ref[...] = sum(bterms)

    return call(
        body,
        [shape((height, width), F32), shape((height, width), BF), shape((height, width), BF)] + [shape((1, width), F32)] * 2,
        name=name,
        flops=2 * height * width * (width + hidden),
    )(hidden_grad, in_weight, grad_out, second, gain, out_weight)


def attend_back(name, limits, queries, pairs, totals, mix, grad_mix, masked):
    array, lead = queries
    _, height, width = array.shape
    size = width // HEADS
    factor = size**-0.5
    count = len(pairs)

    def body(limit_ref, q_ref, total_ref, mix_ref, grad_ref, *refs):
        refs, dq_ref, pair_refs = refs[:count], refs[count], refs[count + 1 :]
        for head in range(HEADS):
            cols = slice(head * size, head * size + size)
            query, grad = q_ref[lead, :, cols], grad_ref[:, cols]
            logged = total_ref[head : head + 1, :] * LOG2E
            delta = jnp.sum(grad.astype(F32) * mix_ref[:, cols], -1, keepdims=True)
            delta = jnp.transpose(jnp.broadcast_to(delta, (height, 128)))[0:1, :]
            dq = None
            for index, ref in enumerate(refs):
                key, value = ref[pairs[index][1], :, cols], ref[pairs[index][2], :, cols]
                prob = jnp.exp2(dot_nt(key, query) * (factor * LOG2E) - logged)
                if masked:
                    place = lax.broadcasted_iota(jnp.int32, prob.shape, 0)
                    prob = jnp.where(place < limit_ref[index], prob, 0.0)
                slope = dot_nt(value, grad)
                pair_refs[index][1, :, cols] = dot(prob.astype(BF), grad).astype(BF)
                ds = (prob * (slope - delta)).astype(BF)
                pair_refs[index][0, :, cols] = (dot(ds, query) * factor).astype(BF)
                piece = dot_tn(ds, key)
                dq = piece if dq is None else dq + piece
            dq_ref[:, cols] = (dq * factor).astype(BF)

    heights = [p[0].shape[1] for p in pairs]
    return call(
        body,
        [shape((height, width), BF)] + [shape((2, keys, width), BF) for keys in heights],
        scalars=1,
        name=name,
        flops=20 * height * sum(heights) * width,
    )(limits, array, totals, mix, grad_mix, *[p[0] for p in pairs])


def norm_grad(name, sources, weights, rows, gain, extra, out_weight, kind):
    height, width = rows.shape
    count = len(sources)
    has_extra, has_out = extra is not None, out_weight is not None
    arrays = []
    for source in sources:
        if not any(source[0] is array for array in arrays):
            arrays.append(source[0])
    where = [[array is source[0] for array in arrays].index(True) for source in sources]

    def body(*refs):
        refs = list(refs)
        source_refs = refs[: len(arrays)]
        weight_ref, rows_ref, gain_ref = refs[len(arrays) : len(arrays) + 3]
        rest = refs[len(arrays) + 3 :]
        extra_ref = rest.pop(0) if has_extra else None
        ow_ref = rest.pop(0) if has_out else None
        grad_ref = rest.pop(0)
        mix_ref = rest.pop(0) if has_out else None
        gterm_ref, bterm_ref = rest
        gterms, bterms = [], []
        for at in pieces(height, 256):
            upstream = None
            for (_, lead, index), place in zip(sources, where):
                ref = source_refs[place]
                piece = dot_nt(ref[at, :] if lead is None else ref[lead, at, :], weight_ref[index])
                upstream = piece if upstream is None else upstream + piece
            grad, gterm, bterm = norm_back(rows_ref[at, :].astype(F32), gain_ref[...], upstream)
            gterms.append(gterm)
            bterms.append(bterm)
            if has_extra:
                grad = grad + extra_ref[at, :].astype(F32)
            grad_ref[at, :] = grad.astype(kind)
            if has_out:
                mix_ref[at, :] = dot_nt(grad.astype(BF), ow_ref[...]).astype(BF)
        gterm_ref[...] = sum(gterms)
        bterm_ref[...] = sum(bterms)

    args = [*arrays, weights, rows, gain] + ([extra] if has_extra else []) + ([out_weight] if has_out else [])
    outs = [shape((height, width), kind)] + ([shape((height, width), BF)] if has_out else [])
    return call(
        body,
        outs + [shape((1, width), F32)] * 2,
        name=name,
        flops=2 * height * width * width * (count + has_out),
    )(*args)


BITS = {"core": ("narrow", 0), "x": ("narrow", 1), "y": ("wide", 0), "z": ("wide", 1), "zz": ("wide", 2)}


def grad_blocks(place, items, order, flip, received, name):
    args, plans, row, scratch, flops = [], [], 0, [], 0

    def add(array):
        for index, had in enumerate(args):
            if had is array:
                return index
        args.append(array)
        return len(args) - 1

    for item in items:
        if item[0] == "outer":
            lefts = [(add(array), lead) for array, lead in item[1]]
            rights = [(add(array), lead) for array, lead in item[2]]
            rows = item[1][0][0].shape[-1] // 4
            cols = item[2][0][0].shape[-1] // 8
            low, high = item[3] if len(item) > 3 else (0, rows if cols < 256 else cols // 128)
            if cols < 256:
                scratch += [pltpu.VMEM((array.shape[-2], 8 * cols), BF) for array, _ in item[2]]
            plans.append(("outer", lefts, rights, (rows, low, high), cols, row))
            here = high - low if cols < 256 else (high - low) * rows
            row += here
            flops += sum(2 * a.shape[-2] * here * 2 * 128 * 8 for a, _ in item[1])
        else:
            array = item[1]
            rows = array.shape[0] // 4 if item[0] == "rows" else array.shape[2]
            plans.append((item[0], add(array), None, rows, 128, row))
            row += rows
    if received is not None:
        args.append(received)
    n_in = len(args)
    later = order[1:]
    spares = len(scratch)
    joined = received is None
    out_shapes = [shape((2, 2, 2, 2, row, 128), BF)] if joined else [shape((2, 2, 2, row, 128), BF)] * 2
    n_out = len(out_shapes)
    copies = 8 * len(plans)

    def body(place_ref, *refs):
        outs = refs[n_in : n_in + n_out]
        turned = refs[n_in + n_out : n_in + n_out + spares]
        buffers, sems = refs[n_in + n_out + spares : n_in + 2 * n_out + spares], refs[n_in + 2 * n_out + spares]
        if joined:
            outs, buffers = [outs[0].at[half] for half in range(2)], [buffers[0].at[half] for half in range(2)]
        narrow_me, wide_me = place_ref[0], place_ref[1]
        flights = []

        def pick(entry):
            return refs[entry[0]] if entry[1] is None else refs[entry[0]].at[entry[1]]

        def put(x, away, first, value):
            bits = {"y": away & 1, "z": (away >> 1) & 1, "zz": away >> 2, "x": x}
            half = bits[order[0]]
            at = (*[bits[bit] for bit in later], slice(first, first + value.shape[0]), slice(None))
            if not joined:
                value = value + buffers[half][at].astype(F32)
            buffers[half][at] = value.astype(BF)

        def fly(x, first, rows):
            for half in range(2):
                if order[0] == "x" and half != x:
                    continue
                at = tuple(x if bit == "x" else slice(None) for bit in later) + (slice(first, first + rows),)
                flight = pltpu.make_async_copy(buffers[half].at[at], outs[half].at[at], sems.at[len(flights)])
                flight.start()
                flights.append(flight)

        arrivals = [[], []]
        for x in range(2):
            for half in range(2):
                if not joined and (order[0] != "x" or half == x):
                    at = tuple(x if bit == "x" else slice(None) for bit in later)
                    source = refs[n_in - 1].at[half]
                    arrival = pltpu.make_async_copy(source.at[at], buffers[half].at[at], sems.at[copies + 2 * x + half])
                    arrival.start()
                    arrivals[x].append(arrival)
        spare = 0
        sorted_refs = {}
        for index, (kind, lefts, rights, rows, cols, first) in enumerate(plans):
            if kind == "outer" and cols < 256:
                sorted_refs[index] = turned[spare : spare + len(rights)]
                for entry, target in zip(rights, sorted_refs[index]):
                    for away in range(8):
                        columns = pl.ds(pl.multiple_of((wide_me ^ away) * cols, cols), cols)
                        target[:, away * cols : away * cols + cols] = pick(entry)[:, columns]
                spare += len(rights)
        for x in range(2):
            narrow = narrow_me ^ (2 * x + flip)
            for arrival in arrivals[x]:
                arrival.wait()
            for index, (kind, lefts, rights, rows, cols, first) in enumerate(plans):
                if kind == "outer":
                    rows, low, high = rows
                if kind == "outer" and cols < 256:
                    half = low + ((high - low) // 256 * 128 if high - low > 512 else high - low)
                    for top, end in ((low, half), (half, high)):
                        tile = end - top
                        if not tile:
                            continue
                        columns = pl.ds(pl.multiple_of(narrow * rows + top, 128), tile)
                        product = sum(
                            dot_tn(pick(entry)[:, columns], b[...]) for entry, b in zip(lefts, sorted_refs[index])
                        )
                        for away in range(8):
                            put(x, away, first + top - low, product[:, away * cols : away * cols + cols])
                        fly(x, first + top - low, tile)
                elif kind == "outer":
                    left = pl.ds(pl.multiple_of(narrow * rows, rows), rows)
                    for away in range(8):
                        columns = pl.ds(pl.multiple_of((wide_me ^ away) * cols + low * 128, 128), (high - low) * 128)
                        product = sum(dot_tn(pick(a)[:, left], pick(b)[:, columns]) for a, b in zip(lefts, rights))
                        for part in range(high - low):
                            put(x, away, first + part * rows, product[:, part * 128 : part * 128 + 128])
                    fly(x, first, rows * (high - low))
                elif kind == "rows":
                    here = pl.ds(pl.multiple_of(narrow * rows, rows), rows)
                    for away in range(8):
                        columns = pl.ds(pl.multiple_of((wide_me ^ away) * 128, 128), 128)
                        put(x, away, first, refs[lefts][here, columns].astype(F32))
                    fly(x, first, rows)
                else:
                    for away in range(8):
                        put(x, away, first, refs[lefts][narrow, wide_me ^ away].astype(F32))
                    fly(x, first, rows)
        for flight in flights:
            flight.wait()

    return call(
        body,
        out_shapes,
        scratch=[*scratch, *[pltpu.VMEM(out.shape, BF) for out in out_shapes], pltpu.SemaphoreType.DMA((copies + 4,))],
        scalars=1,
        flops=flops,
        limit=24,
        outs_far=True,
        last_far=not joined,
        name=name,
    )(place, *args)


def swap(value, bit):
    axis, index = BITS[bit]
    pairs = [(source, source ^ (1 << index)) for source in range(lax.axis_size(axis))]
    return lax.ppermute(value, axis, pairs)


PARTS = {
    "a": "out:0-1024",
    "b": "in:0-4",
    "d": "self_out self_q",
    "e": "self_k self_v",
    "f": "cross_k cross_v",
    "g": "cross_out cross_q rows ready",
}
STEPS = {
    "a": "z x y zz",
    "b": "y z x zz",
    "d": "x y z zz",
    "f": "y z x zz",
    "g": "x y z zz",
    "e": "z y x zz",
}
SCHEDULE = (
    "queries", "kept_keys", "cross_kept", "expand", "other_keys", "cross", "middle", "inner",
    "hidden", "<a", "second", "<b", ">a", ">b", "inner_back", "first", "cross_back", "<f", "<d", "learned", "a~",
    "own", "a~", "<e", "b", "give", "!", "<g", ">e", ">d", "result", "b", ">f", ">g", "d~", "e~", "=", "a", "|", "d", "e", "g", "b", "f~", "|", "f", "g",
    "|",
)


COSTS = {
    "give": 10000000000000,
    "own": 10000000000000,
    "rest": 3,
    "flush": 1000000000000000,
    "cross_back": 100000000000,
    "keep_b": 10000000000000,
}


class Values:
    pass


def gate(name):
    call(lambda: None, [], name=name, limit=4)()


class Reduction:
    def __init__(self, place, order, name):
        self.place, self.order, self.name = place, order, name

    def send(self, items):
        self.items = items
        self.arrived = swap(grad_blocks(self.place, items, self.order, 1, None, "send_" + self.name)[0], "core")

    def keep(self):
        kept, sent = grad_blocks(self.place, self.items, self.order, 0, self.arrived, "keep_" + self.name)
        self.parts = [kept, swap(sent, self.order[0])]

    def step(self, pinned=False):
        bit = self.order[len(self.parts) - 1]
        sent = (total_of([part[1] for part in self.parts]) + Order.token[0]).astype(BF)
        self.parts = [part[0] for part in self.parts] + [swap(sent, bit)]
        if pinned:
            Order.last.append(pltpu.with_memory_space_constraint(sent, pltpu.HBM))

    def finish(self):
        while len(self.parts) <= len(self.order):
            self.step()
        return total_of(self.parts)


def total_of(parts):
    return sum(part.astype(F32) for part in parts)


def outer_sum(lefts, rights):
    return sum(lax.dot_general(a, b, dims(0, 0), preferred_element_type=F32) for a, b in zip(lefts, rights))


def to_blocks(term, wide_count, narrow_count):
    lead, rows, cols = term.shape
    split = term.reshape(lead, narrow_count, rows // narrow_count, wide_count, cols // wide_count)
    moved = jnp.transpose(split, (3, 1, 0, 2, 4))
    return moved.reshape(wide_count * narrow_count, lead, rows // narrow_count, cols // wide_count)


def from_partner(value, axis, bit):
    mask = 2**bit
    pairs = [(source, source ^ mask) for source in range(lax.axis_size(axis))]
    return lax.ppermute(value, axis, pairs)


def on_device(
    tokens,
    lengths,
    latents,
    norm_gain,
    norm_bias,
    cross_qkv,
    cross_out,
    self_qkv,
    self_out,
    mlp_in,
    mlp_biases,
    mlp_out,
    cotangent,
):
    Order.last = []
    half_rows = tokens.shape[1] // 2
    width = tokens.shape[2]
    hidden_width = mlp_in.shape[1]
    wide_size = lax.axis_size("wide")
    narrow_size = lax.axis_size("narrow")
    wide_me = lax.axis_index("wide")
    narrow_me = lax.axis_index("narrow")
    place = jnp.stack([narrow_me, wide_me]).astype(jnp.int32)
    leader = wide_me < wide_size // 2
    partner_bit = wide_size.bit_length() - 2
    own_rows = tokens[0]
    outgoing = lax.dynamic_slice(own_rows, (jnp.where(leader, half_rows, 0), 0), (half_rows, width))
    incoming = from_partner(outgoing, "wide", partner_bit)
    kept = lax.dynamic_slice(own_rows, (jnp.where(leader, 0, half_rows), 0), (half_rows, width))
    length = jnp.where(leader, lengths[0, 0], lengths[0, 1])
    limits = jnp.stack([jnp.where(leader, length, length - half_rows), jnp.where(leader, length - half_rows, length)])
    gains = [norm_gain[i : i + 1] for i in range(4)]
    shifts = [norm_bias[i : i + 1] for i in range(4)]
    inner_bias = mlp_biases[None, :hidden_width]
    outer_bias = mlp_biases[None, hidden_width:]
    grad_out = cotangent[0]

    fast = (narrow_size, wide_size) == (4, 8)
    cut = 5 * (hidden_width // narrow_size) // 8
    sums = {name: Reduction(place, order.split(), name) for name, order in STEPS.items()}
    n = Values()

    def outer(lefts, rights, *limits):
        entry = lambda value: value if isinstance(value, tuple) else (value, None)
        return ("outer", [entry(left) for left in lefts], [entry(right) for right in rights], *limits)

    def queries():
        n.latent_low, n.query = project("queries", latents, gains[1], shifts[1], cross_qkv, 0, 1)

    def kept_keys():
        n.kept_low, n.kept_kv = project("kept", kept, gains[0], shifts[0], cross_qkv, 1, 2)

    def expand():
        n.grad_act, n.grad_out_bias = expand_grad("expand", grad_out, mlp_out)

    def other_keys():
        n.other_low, n.other_kv = project("other", incoming, gains[0], shifts[0], cross_qkv, 1, 2)
        n.pairs = [(n.kept_kv, 0, 1), (n.other_kv, 0, 1)]

    def cross_kept():
        n.part = attend("cross_kept", limits[:1], (n.query, 0), [(n.kept_kv, 0, 1)], True, None, False)

    def cross():
        n.cross_mix, n.cross_total, n.cross_full = attend(
            "cross", limits[1:], (n.query, 0), [(n.other_kv, 0, 1)], True, n.part
        )

    def middle():
        n.first_sum, n.self_low, n.self_q = mix_project(
            "middle", n.cross_mix, cross_out, latents, gains[2], shifts[2], self_qkv
        )
        n.self_pairs = [(n.self_q, 1, 2)]

    def inner():
        n.self_mix, n.self_total, n.self_full = attend("inner", limits, (n.self_q, 0), n.self_pairs, False)

    def hidden():
        n.second_sum, n.mlp_low, n.active, n.hidden_low, n.grad_mlp_bias = mlp_hidden(
            "hidden", n.self_mix, self_out, n.first_sum, gains[3], shifts[3], mlp_in, inner_bias, n.grad_act
        )

    def result():
        n.result = mlp_result("result", n.active, mlp_out, outer_bias, n.second_sum)

    def second():
        n.grad_second, n.second_low, n.grad_self_mix, n.gain_mlp, n.shift_mlp = second_grad(
            "second", n.hidden_low, mlp_in, grad_out, n.second_sum, gains[3], self_out
        )

    def inner_back():
        n.self_gq, n.self_gkv = attend_back(
            "inner_back", limits, (n.self_q, 0), n.self_pairs, n.self_total, n.self_full, n.grad_self_mix, False
        )

    def first():
        n.first_low, n.grad_cross_mix, n.gain_self, n.shift_self = norm_grad(
            "first",
            [(n.self_gq, None, 0), (n.self_gkv, 0, 1), (n.self_gkv, 1, 2)],
            self_qkv,
            n.first_sum,
            gains[2],
            n.grad_second,
            cross_out,
            BF,
        )

    def cross_back():
        n.cross_gq, n.kept_gkv, n.other_gkv = attend_back(
            "cross_back", limits, (n.query, 0), n.pairs, n.cross_total, n.cross_full, n.grad_cross_mix, True
        )

    def give():
        back_sent, n.gain_other, n.shift_other = norm_grad(
            "give", [(n.other_gkv, 0, 1), (n.other_gkv, 1, 2)], cross_qkv, incoming, gains[0], None, None, BF
        )
        n.returned = from_partner(back_sent, "wide", partner_bit)

    def own():
        n.grad_kept, n.gain_kept, n.shift_kept = norm_grad(
            "own", [(n.kept_gkv, 0, 1), (n.kept_gkv, 1, 2)], cross_qkv, kept, gains[0], None, None, F32
        )

    def learned():
        n.grad_latents, n.gain_latent, n.shift_latent = norm_grad(
            "learned", [(n.cross_gq, None, 0)], cross_qkv, latents, gains[1], n.first_low, None, BF
        )

    def terms():
        gain_terms = jnp.concatenate([n.gain_kept + n.gain_other, n.gain_latent, n.gain_self, n.gain_mlp])
        bias_terms = jnp.concatenate([n.shift_kept + n.shift_other, n.shift_latent, n.shift_self, n.shift_mlp])
        return gain_terms, bias_terms, jnp.concatenate([n.grad_mlp_bias, n.grad_out_bias], 1)[0]

    def small():
        gain_terms, bias_terms, bias_vector = terms()
        per_bias = bias_vector.size // (wide_size * narrow_size)
        biases = jnp.transpose(bias_vector.reshape(8, 4, per_bias), (1, 0, 2))
        biases = jnp.pad(biases, ((0, 0), (0, 0), (0, 14 * 128 - per_bias))).reshape(4, 8, 14, 128)
        return jnp.concatenate([gain_terms.reshape(4, 8, 1, 128), bias_terms.reshape(4, 8, 1, 128), biases], 2)

    kinds = {
        "out": lambda *limits: outer([n.active], [grad_out], *limits),
        "in": lambda *limits: outer([n.mlp_low], [n.hidden_low], *limits),
        "self_out": lambda: outer([n.self_mix], [n.second_low]),
        "self_q": lambda: outer([n.self_low], [n.self_gq]),
        "self_k": lambda: outer([n.self_low], [(n.self_gkv, 0)]),
        "self_v": lambda: outer([n.self_low], [(n.self_gkv, 1)]),
        "cross_out": lambda: outer([n.cross_mix], [n.first_low]),
        "cross_q": lambda: outer([n.latent_low], [n.cross_gq]),
        "cross_k": lambda: outer([n.kept_low, n.other_low], [(n.kept_gkv, 0), (n.other_gkv, 0)]),
        "cross_v": lambda: outer([n.kept_low, n.other_low], [(n.kept_gkv, 1), (n.other_gkv, 1)]),
        "rows": lambda: ("rows", n.grad_latents),
        "ready": lambda: ("ready", small()),
    }
    stages = [
        queries, kept_keys, cross_kept, expand, other_keys, cross, middle, inner, hidden, second, inner_back, first, cross_back, give, own,
        learned, result,
    ]
    stages = {stage.__name__: stage for stage in stages}
    for name in SCHEDULE:
        if name in stages:
            stages[name]()
        elif fast and name[0] == "<":
            parts = [part.split(":") for part in PARTS[name[1:]].split()]
            sums[name[1:]].send([kinds[kind](*[tuple(map(int, span.split("-"))) for span in spans]) for kind, *spans in parts])
        elif fast and name[0] == ">":
            sums[name[1:]].keep()
        elif fast and name in "|!":
            gate("flush" if name == "!" else "gate")
        elif fast and name == "=":
            Order.last.append(pltpu.with_memory_space_constraint(n.returned, pltpu.HBM))
        elif fast:
            sums[name[0]].step(name[-1] != "~")
    if fast:
        blocks = {}
        for name, plan in PARTS.items():
            whole, at = sums[name].finish(), 0
            for part in plan.split():
                kind, *span = part.split(":")
                low, high = map(int, span[0].split("-")) if span else (0, 0)
                size = {"out": high - low, "in": (high - low) * width // 4, "rows": latents.shape[0] // 4, "ready": 16}.get(
                    kind, width // 4
                )
                blocks.setdefault(kind, []).append((low, whole[at : at + size]))
                at += size
        blocks = {kind: [block for _, block in sorted(found, key=lambda pair: pair[0])] for kind, found in blocks.items()}
        join = lambda found: found[0] if len(found) == 1 else jnp.concatenate(found)
        rest = blocks["ready"][0]
        inner_blocks = join(blocks["in"])
        shares = (
            blocks["rows"][0],
            rest[:1],
            rest[1:2],
            jnp.stack([blocks["cross_" + kind][0] for kind in "qkv"]),
            blocks["cross_out"][0],
            jnp.stack([blocks["self_" + kind][0] for kind in "qkv"]),
            blocks["self_out"][0],
            jnp.transpose(inner_blocks.reshape(-1, width // 4, 128), (1, 0, 2)).reshape(width // 4, -1),
            rest[2:].reshape(-1)[: mlp_biases.size // (wide_size * narrow_size)],
            join(blocks["out"]),
        )
    else:
        gain_terms, bias_terms, bias_vector = terms()

        def product(kind):
            _, lefts, rights = kinds[kind]()
            pick = lambda entry: entry[0] if entry[1] is None else entry[0][entry[1]]
            return outer_sum([pick(e) for e in lefts], [pick(e) for e in rights])

        matrices = (
            n.grad_latents.astype(F32)[None],
            gain_terms[None],
            bias_terms[None],
            jnp.stack([product("cross_" + kind) for kind in "qkv"]),
            product("cross_out")[None],
            jnp.stack([product("self_" + kind) for kind in "qkv"]),
            product("self_out")[None],
            product("in")[None],
            product("out")[None],
        )
        blocked = tuple(to_blocks(term, wide_size, narrow_size) for term in matrices) + (
            bias_vector.reshape(wide_size * narrow_size, 1, 1, -1),
        )
        summed = lax.psum_scatter(blocked, AXES, scatter_dimension=0, tiled=True)
        s = tuple(entry[0] for entry in summed)
        shares = (s[0][0], s[1][0], s[2][0], s[3], s[4][0], s[5], s[6][0], s[7][0], s[9].reshape(-1), s[8][0])
    returned = n.returned.astype(F32) + Order.token[0, 0]
    tokens_grad = jnp.where(
        leader, jnp.concatenate([n.grad_kept, returned]), jnp.concatenate([returned, n.grad_kept])
    )
    return (n.result[None], tokens_grad[None], *shares)


def solution(mesh):
    return jax.shard_map(
        on_device,
        mesh=mesh,
        in_specs=(
            P(("wide", "narrow"), None, None),
            P(("wide", "narrow"), None),
            P(),
            P(),
            P(),
            P(),
            P(),
            P(),
            P(),
            P(),
            P(),
            P(),
            P(("wide", "narrow"), None, None),
        ),
        out_specs=(
            P(("wide", "narrow"), None, None),
            P(("wide", "narrow"), None, None),
            P("narrow", "wide"),
            P("narrow", "wide"),
            P("narrow", "wide"),
            P(None, "narrow", "wide"),
            P("narrow", "wide"),
            P(None, "narrow", "wide"),
            P("narrow", "wide"),
            P("narrow", "wide"),
            P(("wide", "narrow")),
            P("narrow", "wide"),
        ),
        check_vma=False,
    )
```
